32 devices in a mesh: tm: 4 (over y, core), space: 8 (over z, x).
Axes of the slice: x: 2, y: 2, z: 4, core: 2. Of those that a mesh axis runs over, the one named last changes fastest.
Arguments:
- node_states: float32 [4, 9, 32768], P('tm', None, 'space'), may hold values from -6 to 6
- strengths: float32 [3, 32768], P(None, 'space'), may hold values from -4 to 4
- start_state: float32 [3, 32768], P(None, 'space'), may hold values from -6 to 6
- lists: int32 [256, 12], replicated, may hold values from 0 to 255, as said below
- counts: int32 [8], replicated, may hold values from 16 to 32, as said below
Outputs:
- new_nodes: float32 [4, 9, 32768], P('tm', None, 'space')
The draws below stay inside these ranges and needn't reach their ends.
Inputs may be any that keep to these rules, and one draw needn't show every extreme that they name: `lists`: every entry names a live block; the entries of one row are distinct; over all rows of one shard, live or not, each other shard has between 1 and 2 distinct blocks named, and some pair of shards reaches 2; a shard's own blocks may be named freely. `counts`: number of live blocks of each shard; slots from that number to 31 hold no particles that matter.
All inputs are finite; a program needn't handle non-finite values.
Results may differ from the reference program's by a relative error of at most 0.00005.
Values sent between devices are 32-bit elements; how exact they have to be, the bound alone decides.
A program may use at most 64 MiB of HBM per device.

```python
import math
import jax
import jax.numpy as jnp
import numpy as np
from jax import lax

BLK = 128
LIST = 12
CAP = 2
BLK_DEV = 32
NBLK = 256
NP = 32768
N_TM = 4
N_SPACE = 8


def shared_lists(key):
    folded = jax.random.fold_in(key, 7)
    streams = jax.random.split(folded, 8)
    shard_ids = jnp.arange(N_SPACE, dtype=jnp.int32)
    counts = jax.random.randint(streams[0], (N_SPACE,), BLK_DEV // 2, BLK_DEV + 1)
    top_rank = jax.random.randint(streams[1], (), 0, N_SPACE)
    low_rank = (top_rank + 1 + jax.random.randint(streams[2], (), 0, N_SPACE - 1)) % N_SPACE
    counts = jnp.where(shard_ids == top_rank, BLK_DEV, counts)
    counts = jnp.where(shard_ids == low_rank, BLK_DEV // 2, counts)
    local_ids = jnp.arange(BLK_DEV, dtype=jnp.int32)
    empty_slot = (local_ids[None, None, :] >= counts[None, :, None]).astype(jnp.int32)
    jitter = jax.random.randint(streams[3], (N_SPACE, N_SPACE, BLK_DEV), 0, 4096)
    ordering = empty_slot * (1 << 24) + jitter * BLK_DEV + local_ids[None, None, :]
    chosen = jnp.argsort(ordering, axis=-1, stable=True)[:, :, :CAP]
    remote = shard_ids[None, :, None] * BLK_DEV + chosen
    per_pair = jax.random.randint(streams[4], (N_SPACE, N_SPACE), 1, CAP + 1)
    pair_recv = jax.random.randint(streams[5], (), 0, N_SPACE)
    pair_send = (pair_recv + 1 + jax.random.randint(streams[6], (), 0, N_SPACE - 1)) % N_SPACE
    per_pair = jnp.where((shard_ids[:, None] == pair_recv) & (shard_ids[None, :] == pair_send), CAP, per_pair)
    slot_ids = jnp.arange(CAP, dtype=jnp.int32)
    remote_ok = (slot_ids[None, None, :] < per_pair[:, :, None]) & (shard_ids[:, None, None] != shard_ids[None, :, None])
    own_ids = shard_ids[:, None] * BLK_DEV + local_ids[None, :]
    own_ok = local_ids[None, :] < counts[:, None]
    candidates = jnp.concatenate([own_ids, remote.reshape(N_SPACE, N_SPACE * CAP)], axis=1)
    usable = jnp.concatenate([own_ok, remote_ok.reshape(N_SPACE, N_SPACE * CAP)], axis=1).astype(jnp.int32)
    span_all = BLK_DEV + N_SPACE * CAP
    places = jnp.arange(span_all, dtype=jnp.int32)
    shuffle = jax.random.randint(streams[7], (N_SPACE, span_all), 0, 4096)
    shuffled = jnp.argsort((1 - usable) * (1 << 24) + shuffle * span_all + places[None, :], axis=-1, stable=True)
    ordered = jnp.take_along_axis(candidates, shuffled, axis=1)
    set_sizes = jnp.sum(usable, axis=1)
    positions = local_ids[:, None] * LIST + jnp.arange(LIST, dtype=jnp.int32)[None, :]
    positions = positions[None] % set_sizes[:, None, None]
    listing = jnp.take_along_axis(ordered, positions.reshape(N_SPACE, BLK_DEV * LIST), axis=1)
    return (listing.reshape(N_SPACE * BLK_DEV, LIST).astype(jnp.int32), counts.astype(jnp.int32))


def draw_lists(key, part):
    return shared_lists(key)[0]


def draw_counts(key, part):
    return shared_lists(key)[1]


def block_scale(rng, dims, cuts, low, largest):
    gain = 1.0
    for dim, parts in cuts:
        heights = jax.random.uniform(jax.random.fold_in(jax.random.fold_in(rng, 6), dim), (parts,), jnp.float32, low / len(cuts), largest / len(cuts))
        gain = gain * jnp.repeat(jnp.exp(heights), dims[dim] // parts).reshape((-1,) + (1,) * (len(dims) - 1 - dim))
    return gain


def scatter_about(rng, extent, spread, most, pieces=(), kind=jnp.bfloat16):
    drawn = spread * jax.random.normal(rng, extent, jnp.float32)
    if pieces:
        drawn = drawn * block_scale(rng, extent, pieces, -0.22, 0.18)
    return jnp.clip(drawn, -most, most).astype(kind)


def setup_inputs(seed: int = 0) -> dict:
    arg_keys = jax.random.split(jax.random.key(seed), 6)
    node_states = scatter_about(arg_keys[0], (N_TM, 9, NP), 1.0, 6.0, ((0, 4), (2, 8)), jnp.float32)
    strengths = scatter_about(arg_keys[1], (3, NP), 0.5, 4.0, ((1, 8),), jnp.float32)
    start_state = scatter_about(arg_keys[2], (3, NP), 1.0, 6.0, ((1, 8),), jnp.float32)
    lists = draw_lists(jax.random.fold_in(arg_keys[5], 71), 0)
    counts = draw_counts(jax.random.fold_in(arg_keys[5], 71), 0)
    return dict(node_states=node_states, strengths=strengths, start_state=start_state, lists=lists, counts=counts)


core_sq = 0.25
step_size = 1.0

def radau_matrix():
    sqrt_six = math.sqrt(6.0)
    return np.array([[(88.0 - 7.0 * sqrt_six) / 360.0, (296.0 - 169.0 * sqrt_six) / 1800.0, (-2.0 + 3.0 * sqrt_six) / 225.0], [(296.0 + 169.0 * sqrt_six) / 1800.0, (88.0 + 7.0 * sqrt_six) / 360.0, (-2.0 - 3.0 * sqrt_six) / 225.0], [(16.0 - sqrt_six) / 36.0, (16.0 + sqrt_six) / 36.0, 1.0 / 9.0]])

def cross_rows(former, latter):
    return jnp.stack([former[:, 1] * latter[:, 2] - former[:, 2] * latter[:, 1], former[:, 2] * latter[:, 0] - former[:, 0] * latter[:, 2], former[:, 0] * latter[:, 1] - former[:, 1] * latter[:, 0]], axis=1)

def block_velocity(targets, sources):
    listed = jnp.transpose(sources, (1, 0, 2)).reshape(12, -1)
    places = listed[:9].reshape(3, 3, -1)
    strength = listed[9:]
    target_pos = targets.reshape(3, 3, -1)
    offset = target_pos[:, :, None, :] - places[:, :, :, None]
    kernel = (lax.optimization_barrier(jnp.sum(offset * offset, axis=1)) + core_sq) ** (-1.5)
    terms = cross_rows(offset, strength[None, :, :, None])
    velocity = lax.optimization_barrier(jnp.sum(kernel[:, None] * terms, axis=2))
    return (velocity * (-0.25 / math.pi)).reshape(9, -1)

def reference(node_states, strengths, start_state, lists, counts):
    slices = node_states.shape[0]
    payload = jnp.concatenate([node_states, jnp.broadcast_to(strengths[None], (slices, 3, strengths.shape[1]))], axis=1)
    blocks = payload.reshape(slices, 12, NBLK, BLK).transpose(0, 2, 1, 3)
    block_ids = jnp.arange(NBLK, dtype=jnp.int32)
    live_mask = block_ids % BLK_DEV < counts[block_ids // BLK_DEV]
    grouped = block_ids.reshape(NBLK // BLK_DEV, BLK_DEV)

    def one_slice(slice_data):

        def one_group(members):
            return jax.vmap(lambda target: block_velocity(slice_data[target, :9], slice_data[lists[target]]))(members)
        return lax.map(one_group, grouped).reshape(NBLK, 9, BLK)
    velocity = lax.map(one_slice, blocks)
    velocity = jnp.where(live_mask[None, :, None, None], velocity, jnp.zeros_like(velocity))
    rates = velocity.transpose(0, 2, 1, 3).reshape(slices, 3, 3, NBLK * BLK)
    table = jnp.asarray(radau_matrix(), jnp.float32)
    quadrature = step_size * jnp.einsum('mj,njcp->nmcp', table, rates, precision=lax.Precision.HIGHEST)
    increment = quadrature[:, 2]
    carried = jnp.concatenate([jnp.zeros_like(increment[:1]), jnp.cumsum(increment, axis=0)[:-1]], axis=0)
    updated = start_state[None, None] + carried[:, None] + quadrature
    return updated.reshape(slices, 9, NBLK * BLK)
```

```python
import functools
import math

import jax
import jax.numpy as jnp
import numpy as np
from jax import lax
from jax.experimental import pallas as pl
from jax.experimental.pallas import tpu as pltpu
from jax.sharding import PartitionSpec as P

core_sq = 0.25
step_size = 1.0
block_size = 128
CAP = 2
feature_rows = 32
weight_rows = 16
chunk_blocks = 8
MESH = pl.DeviceIdType.MESH


def radau_matrix():
    sqrt_six = math.sqrt(6.0)
    return np.array(
        [
            [
                (88.0 - 7.0 * sqrt_six) / 360.0,
                (296.0 - 169.0 * sqrt_six) / 1800.0,
                (-2.0 + 3.0 * sqrt_six) / 225.0,
            ],
            [
                (296.0 + 169.0 * sqrt_six) / 1800.0,
                (88.0 + 7.0 * sqrt_six) / 360.0,
                (-2.0 - 3.0 * sqrt_six) / 225.0,
            ],
            [(16.0 - sqrt_six) / 36.0, (16.0 + sqrt_six) / 36.0, 1.0 / 9.0],
        ]
    )


def cut(value):
    head = value.astype(jnp.bfloat16).astype(jnp.float32)
    return head, value - head


def cut_thrice(value):
    high, rest = cut(value)
    middle, low = cut(rest)
    return high, middle, low


def cross(former, latter):
    return jnp.concatenate(
        [
            former[1:2] * latter[2:3] - former[2:3] * latter[1:2],
            former[2:3] * latter[0:1] - former[0:1] * latter[2:3],
            former[0:1] * latter[1:2] - former[1:2] * latter[0:1],
        ],
        axis=0,
    )


def features(pos):
    high, middle, low = cut_thrice(pos)
    square = jnp.sum(pos * pos, axis=0, keepdims=True)
    ones = jnp.ones((3, pos.shape[1]), jnp.float32)
    rest = jnp.zeros((feature_rows - 24, pos.shape[1]), jnp.float32)
    as_target = [high, high, middle, middle, high, low, ones, *cut_thrice(square), rest]
    as_source = [
        high * -2.0,
        middle * -2.0,
        high * -2.0,
        middle * -2.0,
        low * -2.0,
        high * -2.0,
        *cut_thrice(square + core_sq),
        ones,
        rest,
    ]
    return jnp.concatenate(as_target, axis=0), jnp.concatenate(as_source, axis=0)


def source_weights(pos, strength):
    weights = jnp.concatenate([strength, cross(pos, strength)], axis=0)
    high, low = cut(weights)
    rest = jnp.zeros((weight_rows - 12, pos.shape[1]), jnp.float32)
    return jnp.concatenate([high, low, rest], axis=0)


def kernel(
    n_tm,
    groups,
    table_q,
    small_ref,
    lists_ref,
    x_ref,
    a_ref,
    start_ref,
    live_ref,
    o_ref,
    own,
    stage,
    landed,
    table,
    targets,
    totals,
    inc_out,
    inc_in,
    send_sem,
    recv_sem,
    inc_send_sem,
    inc_recv_sem,
):
    tm, me = lax.axis_index("tm"), lax.axis_index("space")
    columns = x_ref.shape[1]
    blocks = columns // block_size
    list_len = lists_ref.shape[0] // blocks
    n_chunks = blocks // chunk_blocks
    chunk = chunk_blocks * block_size

    barrier = pltpu.get_barrier_semaphore()
    for d in range(1, groups):
        peer = lax.rem(me + d, groups)
        pl.semaphore_signal(barrier, inc=1, device_id=(tm, peer), device_id_type=MESH)
    for d in range(1, n_tm):
        peer = lax.rem(tm + d, n_tm)
        pl.semaphore_signal(barrier, inc=1, device_id=(peer, me), device_id_type=MESH)

    def block_at(index):
        return pl.ds(pl.multiple_of(index * block_size, block_size), block_size)

    for block in range(blocks):
        lanes = slice(block * block_size, (block + 1) * block_size)
        own[block, 0:9] = x_ref[:, lanes]
        own[block, 9:12] = a_ref[:, lanes]
    for d in range(1, groups):
        peer = lax.rem(me + d, groups)
        for k in range(CAP):
            lanes = slice(k * block_size, (k + 1) * block_size)
            stage[d, :, lanes] = own[small_ref[k * groups + peer]]

    pl.semaphore_wait(barrier, groups - 1 + n_tm - 1)

    def sources_copy(d):
        return pltpu.make_async_remote_copy(
            src_ref=stage.at[d],
            dst_ref=landed.at[d],
            send_sem=send_sem.at[d],
            recv_sem=recv_sem.at[d],
            device_id=(tm, lax.rem(me + d, groups)),
            device_id_type=MESH,
        )

    for d in range(1, groups):
        sources_copy(d).start()

    centre = jnp.sum(x_ref[...], axis=1, keepdims=True) * (1.0 / columns)

    def enter(slot, count, pos, strength, node):
        as_target, as_source = features(pos)
        weights = source_weights(pos, strength)
        rows = jnp.concatenate([as_source, weights], axis=0).astype(jnp.bfloat16)
        for k in range(count):
            table[slot + k, node] = rows[:, k * block_size : (k + 1) * block_size]
        return as_target

    own_step = 4

    def enter_own(step, carry):
        span = pl.ds(
            pl.multiple_of(step * own_step * block_size, block_size), own_step * block_size
        )
        for node in range(3):
            rows = slice(3 * node, 3 * node + 3)
            pos = x_ref[rows, span] - centre[rows]
            targets[node, :, span] = enter(
                step * own_step, own_step, pos, a_ref[:, span], node
            )
        return carry

    lax.fori_loop(0, blocks // own_step, enter_own, 0)

    for d in range(1, groups):
        sources_copy(d).wait()

    def enter_landed(step, carry):
        for node in range(3):
            rows = slice(3 * node, 3 * node + 3)
            pos = landed[step, rows, :] - centre[rows]
            slot = blocks + (step - 1) * CAP
            enter(slot, CAP, pos, landed[step, 9:12, :], node)
        return carry

    lax.fori_loop(1, groups, enter_landed, 0)

    def inc_copy(d, part):
        return pltpu.make_async_remote_copy(
            src_ref=inc_out.at[part],
            dst_ref=inc_in.at[d, part],
            send_sem=inc_send_sem.at[d, part],
            recv_sem=inc_recv_sem.at[d, part],
            device_id=(lax.rem(tm + d, n_tm), me),
            device_id_type=MESH,
        )

    def one_block(block, carry):
        slots = [lists_ref[block * list_len + j] for j in range(list_len)]
        here = block_at(block)
        for node in range(3):
            lhs = targets[node, :, here].T.astype(jnp.bfloat16)
            total = jnp.zeros((2 * block_size, weight_rows), jnp.float32)
            for j in range(0, list_len, 2):
                pair = jnp.concatenate(
                    [table[slots[j], node], table[slots[j + 1], node]], axis=1
                )
                distance = jnp.dot(
                    lhs, pair[:feature_rows], preferred_element_type=jnp.float32
                )
                inverse = lax.rsqrt(distance)
                value = inverse * inverse * inverse
                high = value.astype(jnp.bfloat16)
                low = (value - high.astype(jnp.float32)).astype(jnp.bfloat16)
                total += lax.dot_general(
                    jnp.concatenate([high, low], axis=0),
                    pair[feature_rows:],
                    (((1,), (1,)), ((), ())),
                    preferred_element_type=jnp.float32,
                )
            total = total[:block_size] + total[block_size:]
            totals[node, :, here] = total.T
        return carry

    def one_chunk(part, carry):
        lax.fori_loop(part * chunk_blocks, (part + 1) * chunk_blocks, one_block, 0)
        span = pl.ds(pl.multiple_of(part * chunk, block_size), chunk)
        scale = live_ref[:, span] * (-0.25 / math.pi)
        rates = []
        for node in range(3):
            rows = slice(3 * node, 3 * node + 3)
            pos = x_ref[rows, span] - centre[rows]
            sums = totals[node, :, span]
            spread = cross(pos, sums[0:3] + sums[6:9]) - (sums[3:6] + sums[9:12])
            rates.append(spread * scale)
        start = start_ref[:, span]
        for node in range(3):
            quadrature = step_size * (
                table_q[node][0] * rates[0]
                + table_q[node][1] * rates[1]
                + table_q[node][2] * rates[2]
            )
            o_ref[3 * node : 3 * node + 3, span] = start + quadrature
        inc_out[part] = quadrature
        for d in range(1, n_tm):

            @pl.when(tm + d < n_tm)
            def _():
                inc_copy(d, part).start()

        return carry

    lax.fori_loop(0, n_chunks, one_chunk, 0)

    def finish(part, carry):
        span = pl.ds(pl.multiple_of(part * chunk, block_size), chunk)
        for d in range(1, n_tm):

            @pl.when(tm + d < n_tm)
            def _():
                inc_copy(d, part).wait_send()

            @pl.when(tm - d >= 0)
            def _():
                inc_copy(d, part).wait_recv()
                arrived = inc_in[d, part]
                for node in range(3):
                    rows = slice(3 * node, 3 * node + 3)
                    o_ref[rows, span] = o_ref[rows, span] + arrived

        return carry

    lax.fori_loop(0, n_chunks, finish, 0)


def shards(node_states, strengths, start_state, lists, counts):
    n_tm, groups = lax.axis_size("tm"), lax.axis_size("space")
    me = lax.axis_index("space")
    blocks = lists.shape[0] // groups
    columns = node_states.shape[2]
    n_chunks = blocks // chunk_blocks
    slots = blocks + (groups - 1) * CAP

    by_shard = lists.reshape(groups, -1)
    owner = by_shard // blocks
    local = by_shard - me * blocks
    asked = owner == me
    first = jnp.min(jnp.where(asked, local, blocks - 1), axis=1)
    last = jnp.max(jnp.where(asked, local, 0), axis=1)
    my_lists = lax.dynamic_index_in_dim(by_shard, me, 0, keepdims=False)
    shard_ids = jnp.arange(groups, dtype=jnp.int32)[:, None]
    lowest = jnp.min(
        jnp.where(my_lists[None] // blocks == shard_ids, my_lists[None], lists.shape[0]), axis=1
    )
    small = jnp.concatenate([first, last])
    shard = my_lists // blocks
    low = jnp.sum(jnp.where(shard[None] == shard_ids, lowest[:, None], 0), axis=0)
    away = (me - shard + groups) % groups
    my_slots = jnp.where(
        shard == me,
        my_lists - me * blocks,
        blocks + (away - 1) * CAP + (my_lists != low).astype(jnp.int32),
    )
    live_count = lax.dynamic_index_in_dim(counts, me, 0, keepdims=False)
    live = jnp.arange(columns, dtype=jnp.int32)[None] < live_count * block_size

    chunk = chunk_blocks * block_size
    out = pl.pallas_call(
        functools.partial(kernel, n_tm, groups, radau_matrix().tolist()),
        out_shape=jax.ShapeDtypeStruct((9, columns), jnp.float32),
        in_specs=[pl.BlockSpec(memory_space=pltpu.SMEM)] * 2
        + [pl.BlockSpec(memory_space=pltpu.VMEM)] * 4,
        out_specs=pl.BlockSpec(memory_space=pltpu.VMEM),
        scratch_shapes=[
            pltpu.VMEM((blocks, 12, block_size), jnp.float32),
            pltpu.VMEM((groups, 12, CAP * block_size), jnp.float32),
            pltpu.VMEM((groups, 12, CAP * block_size), jnp.float32),
            pltpu.VMEM((slots, 3, feature_rows + weight_rows, block_size), jnp.bfloat16),
            pltpu.VMEM((3, feature_rows, columns), jnp.float32),
            pltpu.VMEM((3, weight_rows, columns), jnp.float32),
            pltpu.VMEM((n_chunks, 3, chunk), jnp.float32),
            pltpu.VMEM((n_tm, n_chunks, 3, chunk), jnp.float32),
            pltpu.SemaphoreType.DMA((groups,)),
            pltpu.SemaphoreType.DMA((groups,)),
            pltpu.SemaphoreType.DMA((n_tm, n_chunks)),
            pltpu.SemaphoreType.DMA((n_tm, n_chunks)),
        ],
        compiler_params=pltpu.CompilerParams(
            collective_id=0, has_side_effects=True, vmem_limit_bytes=40 << 20
        ),
        name="vortex_window",
    )(small, my_slots, node_states[0], strengths, start_state, live.astype(jnp.float32))
    return out.reshape(1, 9, -1)


def solution(mesh):
    return jax.shard_map(
        shards,
        mesh=mesh,
        in_specs=(P("tm", None, "space"), P(None, "space"), P(None, "space"), P(), P()),
        out_specs=P("tm", None, "space"),
        check_vma=False,
    )
```

```python
import functools
import math

import jax
import jax.numpy as jnp
import numpy as np
from jax import lax
from jax.experimental import pallas as pl
from jax.experimental.pallas import tpu as pltpu
from jax.sharding import PartitionSpec as P

core_sq = 0.25
step_size = 1.0
block_size = 128
CAP = 2
feature_rows = 32
weight_rows = 16
chunk_blocks = 8
MESH = pl.DeviceIdType.MESH


def radau_matrix():
    sqrt_six = math.sqrt(6.0)
    return np.array(
        [
            [
                (88.0 - 7.0 * sqrt_six) / 360.0,
                (296.0 - 169.0 * sqrt_six) / 1800.0,
                (-2.0 + 3.0 * sqrt_six) / 225.0,
            ],
            [
                (296.0 + 169.0 * sqrt_six) / 1800.0,
                (88.0 + 7.0 * sqrt_six) / 360.0,
                (-2.0 - 3.0 * sqrt_six) / 225.0,
            ],
            [(16.0 - sqrt_six) / 36.0, (16.0 + sqrt_six) / 36.0, 1.0 / 9.0],
        ]
    )


def cut(value):
    head = value.astype(jnp.bfloat16).astype(jnp.float32)
    return head, value - head


def cut_thrice(value):
    high, rest = cut(value)
    middle, low = cut(rest)
    return high, middle, low


def cross(former, latter):
    return jnp.concatenate(
        [
            former[1:2] * latter[2:3] - former[2:3] * latter[1:2],
            former[2:3] * latter[0:1] - former[0:1] * latter[2:3],
            former[0:1] * latter[1:2] - former[1:2] * latter[0:1],
        ],
        axis=0,
    )


def features(pos):
    high, middle, low = cut_thrice(pos)
    square = jnp.sum(pos * pos, axis=0, keepdims=True)
    ones = jnp.ones((3, pos.shape[1]), jnp.float32)
    rest = jnp.zeros((feature_rows - 24, pos.shape[1]), jnp.float32)
    as_target = [high, high, middle, middle, high, low, ones, *cut_thrice(square), rest]
    as_source = [
        high * -2.0,
        middle * -2.0,
        high * -2.0,
        middle * -2.0,
        low * -2.0,
        high * -2.0,
        *cut_thrice(square + core_sq),
        ones,
        rest,
    ]
    return jnp.concatenate(as_target, axis=0), jnp.concatenate(as_source, axis=0)


def source_weights(pos, strength):
    weights = jnp.concatenate([strength, cross(pos, strength)], axis=0)
    high, low = cut(weights)
    rest = jnp.zeros((weight_rows - 12, pos.shape[1]), jnp.float32)
    return jnp.concatenate([high, low, rest], axis=0)


def kernel(
    n_tm,
    groups,
    table_q,
    small_ref,
    lists_ref,
    x_ref,
    a_ref,
    start_ref,
    live_ref,
    o_ref,
    own,
    stage,
    landed,
    table,
    targets,
    parts,
    totals,
    inc_out,
    inc_in,
    send_sem,
    recv_sem,
    inc_send_sem,
    inc_recv_sem,
):
    tm, me = lax.axis_index("tm"), lax.axis_index("space")
    columns = x_ref.shape[1]
    blocks = columns // block_size
    list_len = lists_ref.shape[0] // blocks
    n_chunks = blocks // chunk_blocks
    chunk = chunk_blocks * block_size

    barrier = pltpu.get_barrier_semaphore()
    for d in range(1, groups):
        peer = lax.rem(me + d, groups)
        pl.semaphore_signal(barrier, inc=1, device_id=(tm, peer), device_id_type=MESH)
    for d in range(1, n_tm):
        peer = lax.rem(tm + d, n_tm)
        pl.semaphore_signal(barrier, inc=1, device_id=(peer, me), device_id_type=MESH)

    def block_at(index):
        return pl.ds(pl.multiple_of(index * block_size, block_size), block_size)

    for block in range(blocks):
        lanes = slice(block * block_size, (block + 1) * block_size)
        own[block, 0:9] = x_ref[:, lanes]
        own[block, 9:12] = a_ref[:, lanes]
    for d in range(1, groups):
        peer = lax.rem(me + d, groups)
        for k in range(CAP):
            lanes = slice(k * block_size, (k + 1) * block_size)
            stage[d, :, lanes] = own[small_ref[k * groups + peer]]

    pl.semaphore_wait(barrier, groups - 1 + n_tm - 1)

    def sources_copy(d):
        return pltpu.make_async_remote_copy(
            src_ref=stage.at[d],
            dst_ref=landed.at[d],
            send_sem=send_sem.at[d],
            recv_sem=recv_sem.at[d],
            device_id=(tm, lax.rem(me + d, groups)),
            device_id_type=MESH,
        )

    for d in range(1, groups):
        sources_copy(d).start()

    centre = jnp.sum(x_ref[...], axis=1, keepdims=True) * (1.0 / columns)

    def enter(slot, count, pos, strength, node):
        as_target, as_source = features(pos)
        weights = source_weights(pos, strength)
        rows = jnp.concatenate([as_source, weights], axis=0).astype(jnp.bfloat16)
        for k in range(count):
            table[slot + k, node] = rows[:, k * block_size : (k + 1) * block_size]
        return as_target

    own_step = 4

    def enter_own(step, carry):
        span = pl.ds(
            pl.multiple_of(step * own_step * block_size, block_size), own_step * block_size
        )
        for node in range(3):
            rows = slice(3 * node, 3 * node + 3)
            pos = x_ref[rows, span] - centre[rows]
            targets[node, :, span] = enter(
                step * own_step, own_step, pos, a_ref[:, span], node
            )
        return carry

    lax.fori_loop(0, blocks // own_step, enter_own, 0)

    for d in range(1, groups):
        sources_copy(d).wait()

    def enter_landed(step, carry):
        for node in range(3):
            rows = slice(3 * node, 3 * node + 3)
            pos = landed[step, rows, :] - centre[rows]
            slot = blocks + (step - 1) * CAP
            enter(slot, CAP, pos, landed[step, 9:12, :], node)
        return carry

    lax.fori_loop(1, groups, enter_landed, 0)

    def inc_copy(d, part):
        return pltpu.make_async_remote_copy(
            src_ref=inc_out.at[part],
            dst_ref=inc_in.at[d, part],
            send_sem=inc_send_sem.at[d, part],
            recv_sem=inc_recv_sem.at[d, part],
            device_id=(lax.rem(tm + d, n_tm), me),
            device_id_type=MESH,
        )

    def one_block(block, carry):
        slots = [lists_ref[block * list_len + j] for j in range(list_len)]
        here = block_at(block)
        for node in range(3):
            lhs = targets[node, :, here].T.astype(jnp.bfloat16)
            weights = []
            for j in range(0, list_len, 2):
                pair = jnp.concatenate(
                    [table[slots[j], node], table[slots[j + 1], node]], axis=1
                )
                distance = jnp.dot(
                    lhs, pair[:feature_rows], preferred_element_type=jnp.float32
                )
                inverse = lax.rsqrt(distance)
                value = inverse * inverse * inverse
                high = value.astype(jnp.bfloat16)
                low = (value - high.astype(jnp.float32)).astype(jnp.bfloat16)
                lanes = slice(j * block_size, (j + 2) * block_size)
                parts[node, :block_size, lanes] = high
                parts[node, block_size:, lanes] = low
                weights.append(pair[feature_rows:])
            total = lax.dot_general(
                parts[node],
                jnp.concatenate(weights, axis=1),
                (((1,), (1,)), ((), ())),
                preferred_element_type=jnp.float32,
            )
            total = total[:block_size] + total[block_size:]
            totals[node, :, here] = total.T
        return carry

    def one_chunk(part, carry):
        lax.fori_loop(part * chunk_blocks, (part + 1) * chunk_blocks, one_block, 0)
        span = pl.ds(pl.multiple_of(part * chunk, block_size), chunk)
        scale = live_ref[:, span] * (-0.25 / math.pi)
        rates = []
        for node in range(3):
            rows = slice(3 * node, 3 * node + 3)
            pos = x_ref[rows, span] - centre[rows]
            sums = totals[node, :, span]
            spread = cross(pos, sums[0:3] + sums[6:9]) - (sums[3:6] + sums[9:12])
            rates.append(spread * scale)
        start = start_ref[:, span]
        for node in range(3):
            quadrature = step_size * (
                table_q[node][0] * rates[0]
                + table_q[node][1] * rates[1]
                + table_q[node][2] * rates[2]
            )
            o_ref[3 * node : 3 * node + 3, span] = start + quadrature
        inc_out[part] = quadrature
        for d in range(1, n_tm):

            @pl.when(tm + d < n_tm)
            def _():
                inc_copy(d, part).start()

        return carry

    lax.fori_loop(0, n_chunks, one_chunk, 0)

    def finish(part, carry):
        span = pl.ds(pl.multiple_of(part * chunk, block_size), chunk)
        for d in range(1, n_tm):

            @pl.when(tm + d < n_tm)
            def _():
                inc_copy(d, part).wait_send()

            @pl.when(tm - d >= 0)
            def _():
                inc_copy(d, part).wait_recv()
                arrived = inc_in[d, part]
                for node in range(3):
                    rows = slice(3 * node, 3 * node + 3)
                    o_ref[rows, span] = o_ref[rows, span] + arrived

        return carry

    lax.fori_loop(0, n_chunks, finish, 0)


def shards(node_states, strengths, start_state, lists, counts):
    n_tm, groups = lax.axis_size("tm"), lax.axis_size("space")
    me = lax.axis_index("space")
    blocks = lists.shape[0] // groups
    columns = node_states.shape[2]
    n_chunks = blocks // chunk_blocks
    slots = blocks + (groups - 1) * CAP

    by_shard = lists.reshape(groups, -1)
    owner = by_shard // blocks
    local = by_shard - me * blocks
    asked = owner == me
    first = jnp.min(jnp.where(asked, local, blocks - 1), axis=1)
    last = jnp.max(jnp.where(asked, local, 0), axis=1)
    my_lists = lax.dynamic_index_in_dim(by_shard, me, 0, keepdims=False)
    shard_ids = jnp.arange(groups, dtype=jnp.int32)[:, None]
    lowest = jnp.min(
        jnp.where(my_lists[None] // blocks == shard_ids, my_lists[None], lists.shape[0]), axis=1
    )
    small = jnp.concatenate([first, last])
    shard = my_lists // blocks
    low = jnp.sum(jnp.where(shard[None] == shard_ids, lowest[:, None], 0), axis=0)
    away = (me - shard + groups) % groups
    my_slots = jnp.where(
        shard == me,
        my_lists - me * blocks,
        blocks + (away - 1) * CAP + (my_lists != low).astype(jnp.int32),
    )
    live_count = lax.dynamic_index_in_dim(counts, me, 0, keepdims=False)
    live = jnp.arange(columns, dtype=jnp.int32)[None] < live_count * block_size

    chunk = chunk_blocks * block_size
    out = pl.pallas_call(
        functools.partial(kernel, n_tm, groups, radau_matrix().tolist()),
        out_shape=jax.ShapeDtypeStruct((9, columns), jnp.float32),
        in_specs=[pl.BlockSpec(memory_space=pltpu.SMEM)] * 2
        + [pl.BlockSpec(memory_space=pltpu.VMEM)] * 4,
        out_specs=pl.BlockSpec(memory_space=pltpu.VMEM),
        scratch_shapes=[
            pltpu.VMEM((blocks, 12, block_size), jnp.float32),
            pltpu.VMEM((groups, 12, CAP * block_size), jnp.float32),
            pltpu.VMEM((groups, 12, CAP * block_size), jnp.float32),
            pltpu.VMEM((slots, 3, feature_rows + weight_rows, block_size), jnp.bfloat16),
            pltpu.VMEM((3, feature_rows, columns), jnp.float32),
            pltpu.VMEM((3, 2 * block_size, lists.shape[1] * block_size), jnp.bfloat16),
            pltpu.VMEM((3, weight_rows, columns), jnp.float32),
            pltpu.VMEM((n_chunks, 3, chunk), jnp.float32),
            pltpu.VMEM((n_tm, n_chunks, 3, chunk), jnp.float32),
            pltpu.SemaphoreType.DMA((groups,)),
            pltpu.SemaphoreType.DMA((groups,)),
            pltpu.SemaphoreType.DMA((n_tm, n_chunks)),
            pltpu.SemaphoreType.DMA((n_tm, n_chunks)),
        ],
        compiler_params=pltpu.CompilerParams(
            collective_id=0, has_side_effects=True, vmem_limit_bytes=40 << 20
        ),
        name="vortex_window",
    )(small, my_slots, node_states[0], strengths, start_state, live.astype(jnp.float32))
    return out.reshape(1, 9, -1)


def solution(mesh):
    return jax.shard_map(
        shards,
        mesh=mesh,
        in_specs=(P("tm", None, "space"), P(None, "space"), P(None, "space"), P(), P()),
        out_specs=P("tm", None, "space"),
        check_vma=False,
    )
```

```python
import functools
import math

import jax
import jax.numpy as jnp
import numpy as np
from jax import lax
from jax.experimental import pallas as pl
from jax.experimental.pallas import tpu as pltpu
from jax.sharding import PartitionSpec as P

core_sq = 0.25
step_size = 1.0
block_size = 128
CAP = 2
feature_rows = 32
weight_rows = 16
chunk_blocks = 8
MESH = pl.DeviceIdType.MESH


def radau_matrix():
    sqrt_six = math.sqrt(6.0)
    return np.array(
        [
            [
                (88.0 - 7.0 * sqrt_six) / 360.0,
                (296.0 - 169.0 * sqrt_six) / 1800.0,
                (-2.0 + 3.0 * sqrt_six) / 225.0,
            ],
            [
                (296.0 + 169.0 * sqrt_six) / 1800.0,
                (88.0 + 7.0 * sqrt_six) / 360.0,
                (-2.0 - 3.0 * sqrt_six) / 225.0,
            ],
            [(16.0 - sqrt_six) / 36.0, (16.0 + sqrt_six) / 36.0, 1.0 / 9.0],
        ]
    )


def cut(value):
    head = value.astype(jnp.bfloat16).astype(jnp.float32)
    return head, value - head


def cut_thrice(value):
    high, rest = cut(value)
    middle, low = cut(rest)
    return high, middle, low


def cross(former, latter):
    return jnp.concatenate(
        [
            former[1:2] * latter[2:3] - former[2:3] * latter[1:2],
            former[2:3] * latter[0:1] - former[0:1] * latter[2:3],
            former[0:1] * latter[1:2] - former[1:2] * latter[0:1],
        ],
        axis=0,
    )


def features(pos):
    high, middle, low = cut_thrice(pos)
    square = jnp.sum(pos * pos, axis=0, keepdims=True)
    ones = jnp.ones((3, pos.shape[1]), jnp.float32)
    rest = jnp.zeros((feature_rows - 24, pos.shape[1]), jnp.float32)
    as_target = [high, high, middle, middle, high, low, ones, *cut_thrice(square), rest]
    as_source = [
        high * -2.0,
        middle * -2.0,
        high * -2.0,
        middle * -2.0,
        low * -2.0,
        high * -2.0,
        *cut_thrice(square + core_sq),
        ones,
        rest,
    ]
    return jnp.concatenate(as_target, axis=0), jnp.concatenate(as_source, axis=0)


def source_weights(pos, strength):
    weights = jnp.concatenate([strength, cross(pos, strength)], axis=0)
    high, low = cut(weights)
    rest = jnp.zeros((weight_rows - 12, pos.shape[1]), jnp.float32)
    return jnp.concatenate([high, low, rest], axis=0)


def kernel(
    n_tm,
    groups,
    table_q,
    small_ref,
    lists_ref,
    x_ref,
    a_ref,
    start_ref,
    live_ref,
    o_ref,
    own,
    stage,
    landed,
    table,
    targets,
    parts,
    totals,
    inc_out,
    inc_in,
    send_sem,
    recv_sem,
    inc_send_sem,
    inc_recv_sem,
):
    tm, me = lax.axis_index("tm"), lax.axis_index("space")
    columns = x_ref.shape[1]
    blocks = columns // block_size
    list_len = lists_ref.shape[0] // blocks
    n_chunks = blocks // chunk_blocks
    chunk = chunk_blocks * block_size

    barrier = pltpu.get_barrier_semaphore()
    for d in range(1, groups):
        peer = lax.rem(me + d, groups)
        pl.semaphore_signal(barrier, inc=1, device_id=(tm, peer), device_id_type=MESH)
    for d in range(1, n_tm):
        peer = lax.rem(tm + d, n_tm)
        pl.semaphore_signal(barrier, inc=1, device_id=(peer, me), device_id_type=MESH)

    def block_at(index):
        return pl.ds(pl.multiple_of(index * block_size, block_size), block_size)

    for block in range(blocks):
        lanes = slice(block * block_size, (block + 1) * block_size)
        own[block, 0:9] = x_ref[:, lanes]
        own[block, 9:12] = a_ref[:, lanes]
    for d in range(1, groups):
        peer = lax.rem(me + d, groups)
        for k in range(CAP):
            lanes = slice(k * block_size, (k + 1) * block_size)
            stage[d, :, lanes] = own[small_ref[k * groups + peer]]

    pl.semaphore_wait(barrier, groups - 1 + n_tm - 1)

    def sources_copy(d):
        return pltpu.make_async_remote_copy(
            src_ref=stage.at[d],
            dst_ref=landed.at[d],
            send_sem=send_sem.at[d],
            recv_sem=recv_sem.at[d],
            device_id=(tm, lax.rem(me + d, groups)),
            device_id_type=MESH,
        )

    for d in range(1, groups):
        sources_copy(d).start()

    centre = jnp.sum(x_ref[...], axis=1, keepdims=True) * (1.0 / columns)

    def enter(slot, count, pos, strength):
        here = [pos[3 * node : 3 * node + 3] for node in range(3)]
        pairs = [features(place) for place in here]
        weights = [source_weights(place, strength) for place in here]
        rows = [as_source for _, as_source in pairs] + weights
        rows = jnp.concatenate(rows, axis=0).astype(jnp.bfloat16)
        for k in range(count):
            table[slot + k] = rows[:, k * block_size : (k + 1) * block_size]
        return jnp.concatenate([as_target for as_target, _ in pairs], axis=0)

    own_step = 4

    def enter_own(step, carry):
        span = pl.ds(
            pl.multiple_of(step * own_step * block_size, block_size), own_step * block_size
        )
        pos = x_ref[:, span] - centre
        targets[:, span] = enter(step * own_step, own_step, pos, a_ref[:, span])
        return carry

    lax.fori_loop(0, blocks // own_step, enter_own, 0)

    for d in range(1, groups):
        sources_copy(d).wait()

    def enter_landed(step, carry):
        pos = landed[step, 0:9, :] - centre
        enter(blocks + (step - 1) * CAP, CAP, pos, landed[step, 9:12, :])
        return carry

    lax.fori_loop(1, groups, enter_landed, 0)

    def inc_copy(d, part):
        return pltpu.make_async_remote_copy(
            src_ref=inc_out.at[part],
            dst_ref=inc_in.at[d, part],
            send_sem=inc_send_sem.at[d, part],
            recv_sem=inc_recv_sem.at[d, part],
            device_id=(lax.rem(tm + d, n_tm), me),
            device_id_type=MESH,
        )

    def one_block(block, carry):
        slots = [lists_ref[block * list_len + j] for j in range(list_len)]
        here = block_at(block)
        turned = targets[:, here].T
        node_of = lax.broadcasted_iota(jnp.int32, turned.shape, 1) // feature_rows
        lhs = [jnp.where(node_of == node, turned, 0.0) for node in range(3)]
        lhs = jnp.concatenate(lhs, axis=0).astype(jnp.bfloat16)
        weights = []
        for j in range(0, list_len, 2):
            pair = jnp.concatenate([table[slots[j]], table[slots[j + 1]]], axis=1)
            distance = jnp.dot(
                lhs, pair[: 3 * feature_rows], preferred_element_type=jnp.float32
            )
            inverse = lax.rsqrt(distance)
            value = inverse * inverse * inverse
            high = value.astype(jnp.bfloat16)
            low = (value - high.astype(jnp.float32)).astype(jnp.bfloat16)
            lanes = slice(j * block_size, (j + 2) * block_size)
            parts[: 3 * block_size, lanes] = high
            parts[3 * block_size :, lanes] = low
            weights.append(pair[3 * feature_rows :])
        total = lax.dot_general(
            parts[...],
            jnp.concatenate(weights, axis=1),
            (((1,), (1,)), ((), ())),
            preferred_element_type=jnp.float32,
        )
        total = total[: 3 * block_size] + total[3 * block_size :]
        node_of = lax.broadcasted_iota(jnp.int32, (block_size, 3 * weight_rows), 1) // weight_rows
        kept = jnp.zeros((block_size, 3 * weight_rows), jnp.float32)
        for node in range(3):
            rows = total[node * block_size : (node + 1) * block_size]
            kept = jnp.where(node_of == node, rows, kept)
        totals[:, here] = kept.T
        return carry

    def one_chunk(part, carry):
        lax.fori_loop(part * chunk_blocks, (part + 1) * chunk_blocks, one_block, 0)
        span = pl.ds(pl.multiple_of(part * chunk, block_size), chunk)
        scale = live_ref[:, span] * (-0.25 / math.pi)
        rates = []
        for node in range(3):
            rows = slice(3 * node, 3 * node + 3)
            pos = x_ref[rows, span] - centre[rows]
            sums = totals[weight_rows * node : weight_rows * (node + 1), span]
            spread = cross(pos, sums[0:3] + sums[6:9]) - (sums[3:6] + sums[9:12])
            rates.append(spread * scale)
        start = start_ref[:, span]
        for node in range(3):
            quadrature = step_size * (
                table_q[node][0] * rates[0]
                + table_q[node][1] * rates[1]
                + table_q[node][2] * rates[2]
            )
            o_ref[3 * node : 3 * node + 3, span] = start + quadrature
        inc_out[part] = quadrature
        for d in range(1, n_tm):

            @pl.when(tm + d < n_tm)
            def _():
                inc_copy(d, part).start()

        return carry

    lax.fori_loop(0, n_chunks, one_chunk, 0)

    def finish(part, carry):
        span = pl.ds(pl.multiple_of(part * chunk, block_size), chunk)
        for d in range(1, n_tm):

            @pl.when(tm + d < n_tm)
            def _():
                inc_copy(d, part).wait_send()

            @pl.when(tm - d >= 0)
            def _():
                inc_copy(d, part).wait_recv()
                arrived = inc_in[d, part]
                for node in range(3):
                    rows = slice(3 * node, 3 * node + 3)
                    o_ref[rows, span] = o_ref[rows, span] + arrived

        return carry

    lax.fori_loop(0, n_chunks, finish, 0)


def shards(node_states, strengths, start_state, lists, counts):
    n_tm, groups = lax.axis_size("tm"), lax.axis_size("space")
    me = lax.axis_index("space")
    blocks = lists.shape[0] // groups
    columns = node_states.shape[2]
    n_chunks = blocks // chunk_blocks
    slots = blocks + (groups - 1) * CAP

    by_shard = lists.reshape(groups, -1)
    owner = by_shard // blocks
    local = by_shard - me * blocks
    asked = owner == me
    first = jnp.min(jnp.where(asked, local, blocks - 1), axis=1)
    last = jnp.max(jnp.where(asked, local, 0), axis=1)
    my_lists = lax.dynamic_index_in_dim(by_shard, me, 0, keepdims=False)
    shard_ids = jnp.arange(groups, dtype=jnp.int32)[:, None]
    lowest = jnp.min(
        jnp.where(my_lists[None] // blocks == shard_ids, my_lists[None], lists.shape[0]), axis=1
    )
    small = jnp.concatenate([first, last])
    shard = my_lists // blocks
    low = jnp.sum(jnp.where(shard[None] == shard_ids, lowest[:, None], 0), axis=0)
    away = (me - shard + groups) % groups
    my_slots = jnp.where(
        shard == me,
        my_lists - me * blocks,
        blocks + (away - 1) * CAP + (my_lists != low).astype(jnp.int32),
    )
    live_count = lax.dynamic_index_in_dim(counts, me, 0, keepdims=False)
    live = jnp.arange(columns, dtype=jnp.int32)[None] < live_count * block_size

    chunk = chunk_blocks * block_size
    out = pl.pallas_call(
        functools.partial(kernel, n_tm, groups, radau_matrix().tolist()),
        out_shape=jax.ShapeDtypeStruct((9, columns), jnp.float32),
        in_specs=[pl.BlockSpec(memory_space=pltpu.SMEM)] * 2
        + [pl.BlockSpec(memory_space=pltpu.VMEM)] * 4,
        out_specs=pl.BlockSpec(memory_space=pltpu.VMEM),
        scratch_shapes=[
            pltpu.VMEM((blocks, 12, block_size), jnp.float32),
            pltpu.VMEM((groups, 12, CAP * block_size), jnp.float32),
            pltpu.VMEM((groups, 12, CAP * block_size), jnp.float32),
            pltpu.VMEM((slots, 3 * (feature_rows + weight_rows), block_size), jnp.bfloat16),
            pltpu.VMEM((3 * feature_rows, columns), jnp.float32),
            pltpu.VMEM((6 * block_size, lists.shape[1] * block_size), jnp.bfloat16),
            pltpu.VMEM((3 * weight_rows, columns), jnp.float32),
            pltpu.VMEM((n_chunks, 3, chunk), jnp.float32),
            pltpu.VMEM((n_tm, n_chunks, 3, chunk), jnp.float32),
            pltpu.SemaphoreType.DMA((groups,)),
            pltpu.SemaphoreType.DMA((groups,)),
            pltpu.SemaphoreType.DMA((n_tm, n_chunks)),
            pltpu.SemaphoreType.DMA((n_tm, n_chunks)),
        ],
        compiler_params=pltpu.CompilerParams(
            collective_id=0, has_side_effects=True, vmem_limit_bytes=40 << 20
        ),
        name="vortex_window",
    )(small, my_slots, node_states[0], strengths, start_state, live.astype(jnp.float32))
    return out.reshape(1, 9, -1)


def solution(mesh):
    return jax.shard_map(
        shards,
        mesh=mesh,
        in_specs=(P("tm", None, "space"), P(None, "space"), P(None, "space"), P(), P()),
        out_specs=P("tm", None, "space"),
        check_vma=False,
    )
```

```python
import functools
import math

import jax
import jax.numpy as jnp
import numpy as np
from jax import lax
from jax.experimental import pallas as pl
from jax.experimental.pallas import tpu as pltpu
from jax.sharding import PartitionSpec as P

core_sq = 0.25
step_size = 1.0
block_size = 128
CAP = 2
feature_rows = 32
weight_rows = 16
chunk_blocks = 8
MESH = pl.DeviceIdType.MESH


def radau_matrix():
    sqrt_six = math.sqrt(6.0)
    return np.array(
        [
            [
                (88.0 - 7.0 * sqrt_six) / 360.0,
                (296.0 - 169.0 * sqrt_six) / 1800.0,
                (-2.0 + 3.0 * sqrt_six) / 225.0,
            ],
            [
                (296.0 + 169.0 * sqrt_six) / 1800.0,
                (88.0 + 7.0 * sqrt_six) / 360.0,
                (-2.0 - 3.0 * sqrt_six) / 225.0,
            ],
            [(16.0 - sqrt_six) / 36.0, (16.0 + sqrt_six) / 36.0, 1.0 / 9.0],
        ]
    )


def cut(value):
    head = value.astype(jnp.bfloat16).astype(jnp.float32)
    return head, value - head


def cut_thrice(value):
    high, rest = cut(value)
    middle, low = cut(rest)
    return high, middle, low


def cross(former, latter):
    return jnp.concatenate(
        [
            former[1:2] * latter[2:3] - former[2:3] * latter[1:2],
            former[2:3] * latter[0:1] - former[0:1] * latter[2:3],
            former[0:1] * latter[1:2] - former[1:2] * latter[0:1],
        ],
        axis=0,
    )


def features(pos):
    high, middle, low = cut_thrice(pos)
    square = jnp.sum(pos * pos, axis=0, keepdims=True)
    ones = jnp.ones((3, pos.shape[1]), jnp.float32)
    rest = jnp.zeros((feature_rows - 24, pos.shape[1]), jnp.float32)
    as_target = [high, high, middle, middle, high, low, ones, *cut_thrice(square), rest]
    as_source = [
        high * -2.0,
        middle * -2.0,
        high * -2.0,
        middle * -2.0,
        low * -2.0,
        high * -2.0,
        *cut_thrice(square + core_sq),
        ones,
        rest,
    ]
    return jnp.concatenate(as_target, axis=0), jnp.concatenate(as_source, axis=0)


def source_weights(pos, strength):
    weights = jnp.concatenate([strength, cross(pos, strength)], axis=0)
    high, low = cut(weights)
    rest = jnp.zeros((weight_rows - 12, pos.shape[1]), jnp.float32)
    return jnp.concatenate([high, low, rest], axis=0)


def kernel(
    n_tm,
    groups,
    table_q,
    small_ref,
    lists_ref,
    x_ref,
    a_ref,
    start_ref,
    live_ref,
    o_ref,
    own,
    stage,
    landed,
    table,
    targets,
    parts,
    totals,
    inc_out,
    inc_in,
    send_sem,
    recv_sem,
    inc_send_sem,
    inc_recv_sem,
):
    tm, me = lax.axis_index("tm"), lax.axis_index("space")
    columns = x_ref.shape[1]
    blocks = columns // block_size
    list_len = lists_ref.shape[0] // blocks
    n_chunks = blocks // chunk_blocks
    chunk = chunk_blocks * block_size

    barrier = pltpu.get_barrier_semaphore()
    for d in range(1, groups):
        peer = lax.rem(me + d, groups)
        pl.semaphore_signal(barrier, inc=1, device_id=(tm, peer), device_id_type=MESH)
    for d in range(1, n_tm):
        peer = lax.rem(tm + d, n_tm)
        pl.semaphore_signal(barrier, inc=1, device_id=(peer, me), device_id_type=MESH)

    def block_at(index):
        return pl.ds(pl.multiple_of(index * block_size, block_size), block_size)

    for block in range(blocks):
        lanes = slice(block * block_size, (block + 1) * block_size)
        own[block, 0:9] = x_ref[:, lanes]
        own[block, 9:12] = a_ref[:, lanes]
    for d in range(1, groups):
        peer = lax.rem(me + d, groups)
        for k in range(CAP):
            lanes = slice(k * block_size, (k + 1) * block_size)
            stage[d, :, lanes] = own[small_ref[k * groups + peer]]

    pl.semaphore_wait(barrier, groups - 1 + n_tm - 1)

    def sources_copy(d):
        return pltpu.make_async_remote_copy(
            src_ref=stage.at[d],
            dst_ref=landed.at[d],
            send_sem=send_sem.at[d],
            recv_sem=recv_sem.at[d],
            device_id=(tm, lax.rem(me + d, groups)),
            device_id_type=MESH,
        )

    for d in range(1, groups):
        sources_copy(d).start()

    centre = jnp.sum(x_ref[...], axis=1, keepdims=True) * (1.0 / columns)

    def enter(slot, count, pos, strength):
        here = [pos[3 * node : 3 * node + 3] for node in range(3)]
        pairs = [features(place) for place in here]
        weights = [source_weights(place, strength) for place in here]
        rows = [as_source for _, as_source in pairs] + weights
        rows = jnp.concatenate(rows, axis=0).astype(jnp.bfloat16)
        for k in range(count):
            table[slot + k] = rows[:, k * block_size : (k + 1) * block_size]
        return jnp.concatenate([as_target for as_target, _ in pairs], axis=0)

    own_step = 4

    def enter_own(step, carry):
        span = pl.ds(
            pl.multiple_of(step * own_step * block_size, block_size), own_step * block_size
        )
        pos = x_ref[:, span] - centre
        targets[:, span] = enter(step * own_step, own_step, pos, a_ref[:, span])
        return carry

    lax.fori_loop(0, blocks // own_step, enter_own, 0)

    for d in range(1, groups):
        sources_copy(d).wait()

    def enter_landed(step, carry):
        pos = landed[step, 0:9, :] - centre
        enter(blocks + (step - 1) * CAP, CAP, pos, landed[step, 9:12, :])
        return carry

    lax.fori_loop(1, groups, enter_landed, 0)

    def inc_copy(d, part):
        return pltpu.make_async_remote_copy(
            src_ref=inc_out.at[part],
            dst_ref=inc_in.at[d, part],
            send_sem=inc_send_sem.at[d, part],
            recv_sem=inc_recv_sem.at[d, part],
            device_id=(lax.rem(tm + d, n_tm), me),
            device_id_type=MESH,
        )

    def interact(block, buffer):
        slots = [lists_ref[block * list_len + j] for j in range(list_len)]
        here = block_at(block)
        turned = targets[:, here].T
        node_of = lax.broadcasted_iota(jnp.int32, turned.shape, 1) // feature_rows
        lhs = [jnp.where(node_of == node, turned, 0.0) for node in range(3)]
        lhs = jnp.concatenate(lhs, axis=0).astype(jnp.bfloat16)
        for j in range(0, list_len, 2):
            pair = [table[slot, : 3 * feature_rows] for slot in slots[j : j + 2]]
            distance = jnp.dot(
                lhs, jnp.concatenate(pair, axis=1), preferred_element_type=jnp.float32
            )
            inverse = lax.rsqrt(distance)
            value = inverse * inverse * inverse
            high = value.astype(jnp.bfloat16)
            low = (value - high.astype(jnp.float32)).astype(jnp.bfloat16)
            lanes = slice(j * block_size, (j + 2) * block_size)
            parts[buffer, : 3 * block_size, lanes] = high
            parts[buffer, 3 * block_size :, lanes] = low

    def weigh(block, buffer):
        slots = [lists_ref[block * list_len + j] for j in range(list_len)]
        here = block_at(block)
        weights = [table[slot, 3 * feature_rows :] for slot in slots]
        total = lax.dot_general(
            parts[buffer],
            jnp.concatenate(weights, axis=1),
            (((1,), (1,)), ((), ())),
            preferred_element_type=jnp.float32,
        )
        total = total[: 3 * block_size] + total[3 * block_size :]
        node_of = lax.broadcasted_iota(jnp.int32, (block_size, 3 * weight_rows), 1) // weight_rows
        kept = jnp.zeros((block_size, 3 * weight_rows), jnp.float32)
        for node in range(3):
            rows = total[node * block_size : (node + 1) * block_size]
            kept = jnp.where(node_of == node, rows, kept)
        totals[:, here] = kept.T

    def two_blocks(step, carry):
        interact(2 * step + 1, 1)
        weigh(2 * step, 0)
        interact(jnp.minimum(2 * step + 2, blocks - 1), 0)
        weigh(2 * step + 1, 1)
        return carry

    def one_chunk(part, carry):
        steps = chunk_blocks // 2
        lax.fori_loop(part * steps, (part + 1) * steps, two_blocks, 0)
        span = pl.ds(pl.multiple_of(part * chunk, block_size), chunk)
        scale = live_ref[:, span] * (-0.25 / math.pi)
        rates = []
        for node in range(3):
            rows = slice(3 * node, 3 * node + 3)
            pos = x_ref[rows, span] - centre[rows]
            sums = totals[weight_rows * node : weight_rows * (node + 1), span]
            spread = cross(pos, sums[0:3] + sums[6:9]) - (sums[3:6] + sums[9:12])
            rates.append(spread * scale)
        start = start_ref[:, span]
        for node in range(3):
            quadrature = step_size * (
                table_q[node][0] * rates[0]
                + table_q[node][1] * rates[1]
                + table_q[node][2] * rates[2]
            )
            o_ref[3 * node : 3 * node + 3, span] = start + quadrature
        inc_out[part] = quadrature
        for d in range(1, n_tm):

            @pl.when(tm + d < n_tm)
            def _():
                inc_copy(d, part).start()

        return carry

    interact(0, 0)
    lax.fori_loop(0, n_chunks, one_chunk, 0)

    def finish(part, carry):
        span = pl.ds(pl.multiple_of(part * chunk, block_size), chunk)
        for d in range(1, n_tm):

            @pl.when(tm + d < n_tm)
            def _():
                inc_copy(d, part).wait_send()

            @pl.when(tm - d >= 0)
            def _():
                inc_copy(d, part).wait_recv()
                arrived = inc_in[d, part]
                for node in range(3):
                    rows = slice(3 * node, 3 * node + 3)
                    o_ref[rows, span] = o_ref[rows, span] + arrived

        return carry

    lax.fori_loop(0, n_chunks, finish, 0)


def shards(node_states, strengths, start_state, lists, counts):
    n_tm, groups = lax.axis_size("tm"), lax.axis_size("space")
    me = lax.axis_index("space")
    blocks = lists.shape[0] // groups
    columns = node_states.shape[2]
    n_chunks = blocks // chunk_blocks
    slots = blocks + (groups - 1) * CAP

    by_shard = lists.reshape(groups, -1)
    owner = by_shard // blocks
    local = by_shard - me * blocks
    asked = owner == me
    first = jnp.min(jnp.where(asked, local, blocks - 1), axis=1)
    last = jnp.max(jnp.where(asked, local, 0), axis=1)
    my_lists = lax.dynamic_index_in_dim(by_shard, me, 0, keepdims=False)
    shard_ids = jnp.arange(groups, dtype=jnp.int32)[:, None]
    lowest = jnp.min(
        jnp.where(my_lists[None] // blocks == shard_ids, my_lists[None], lists.shape[0]), axis=1
    )
    small = jnp.concatenate([first, last])
    shard = my_lists // blocks
    low = jnp.sum(jnp.where(shard[None] == shard_ids, lowest[:, None], 0), axis=0)
    away = (me - shard + groups) % groups
    my_slots = jnp.where(
        shard == me,
        my_lists - me * blocks,
        blocks + (away - 1) * CAP + (my_lists != low).astype(jnp.int32),
    )
    live_count = lax.dynamic_index_in_dim(counts, me, 0, keepdims=False)
    live = jnp.arange(columns, dtype=jnp.int32)[None] < live_count * block_size

    chunk = chunk_blocks * block_size
    out = pl.pallas_call(
        functools.partial(kernel, n_tm, groups, radau_matrix().tolist()),
        out_shape=jax.ShapeDtypeStruct((9, columns), jnp.float32),
        in_specs=[pl.BlockSpec(memory_space=pltpu.SMEM)] * 2
        + [pl.BlockSpec(memory_space=pltpu.VMEM)] * 4,
        out_specs=pl.BlockSpec(memory_space=pltpu.VMEM),
        scratch_shapes=[
            pltpu.VMEM((blocks, 12, block_size), jnp.float32),
            pltpu.VMEM((groups, 12, CAP * block_size), jnp.float32),
            pltpu.VMEM((groups, 12, CAP * block_size), jnp.float32),
            pltpu.VMEM((slots, 3 * (feature_rows + weight_rows), block_size), jnp.bfloat16),
            pltpu.VMEM((3 * feature_rows, columns), jnp.float32),
            pltpu.VMEM((2, 6 * block_size, lists.shape[1] * block_size), jnp.bfloat16),
            pltpu.VMEM((3 * weight_rows, columns), jnp.float32),
            pltpu.VMEM((n_chunks, 3, chunk), jnp.float32),
            pltpu.VMEM((n_tm, n_chunks, 3, chunk), jnp.float32),
            pltpu.SemaphoreType.DMA((groups,)),
            pltpu.SemaphoreType.DMA((groups,)),
            pltpu.SemaphoreType.DMA((n_tm, n_chunks)),
            pltpu.SemaphoreType.DMA((n_tm, n_chunks)),
        ],
        compiler_params=pltpu.CompilerParams(
            collective_id=0, has_side_effects=True, vmem_limit_bytes=40 << 20
        ),
        name="vortex_window",
    )(small, my_slots, node_states[0], strengths, start_state, live.astype(jnp.float32))
    return out.reshape(1, 9, -1)


def solution(mesh):
    return jax.shard_map(
        shards,
        mesh=mesh,
        in_specs=(P("tm", None, "space"), P(None, "space"), P(None, "space"), P(), P()),
        out_specs=P("tm", None, "space"),
        check_vma=False,
    )
```

```python
import functools
import math

import jax
import jax.numpy as jnp
import numpy as np
from jax import lax
from jax.experimental import pallas as pl
from jax.experimental.pallas import tpu as pltpu
from jax.sharding import PartitionSpec as P

core_sq = 0.25
step_size = 1.0
block_size = 128
CAP = 2
feature_rows = 32
weight_rows = 16
chunk_blocks = 8
MESH = pl.DeviceIdType.MESH


def radau_matrix():
    sqrt_six = math.sqrt(6.0)
    return np.array(
        [
            [
                (88.0 - 7.0 * sqrt_six) / 360.0,
                (296.0 - 169.0 * sqrt_six) / 1800.0,
                (-2.0 + 3.0 * sqrt_six) / 225.0,
            ],
            [
                (296.0 + 169.0 * sqrt_six) / 1800.0,
                (88.0 + 7.0 * sqrt_six) / 360.0,
                (-2.0 - 3.0 * sqrt_six) / 225.0,
            ],
            [(16.0 - sqrt_six) / 36.0, (16.0 + sqrt_six) / 36.0, 1.0 / 9.0],
        ]
    )


def cut(value):
    head = value.astype(jnp.bfloat16).astype(jnp.float32)
    return head, value - head


def cut_thrice(value):
    high, rest = cut(value)
    middle, low = cut(rest)
    return high, middle, low


def cross(former, latter):
    return jnp.concatenate(
        [
            former[1:2] * latter[2:3] - former[2:3] * latter[1:2],
            former[2:3] * latter[0:1] - former[0:1] * latter[2:3],
            former[0:1] * latter[1:2] - former[1:2] * latter[0:1],
        ],
        axis=0,
    )


def features(pos):
    high, middle, low = cut_thrice(pos)
    square = jnp.sum(pos * pos, axis=0, keepdims=True)
    ones = jnp.ones((3, pos.shape[1]), jnp.float32)
    rest = jnp.zeros((feature_rows - 24, pos.shape[1]), jnp.float32)
    as_target = [high, high, middle, middle, high, low, ones, *cut_thrice(square), rest]
    as_source = [
        high * -2.0,
        middle * -2.0,
        high * -2.0,
        middle * -2.0,
        low * -2.0,
        high * -2.0,
        *cut_thrice(square + core_sq),
        ones,
        rest,
    ]
    return jnp.concatenate(as_target, axis=0), jnp.concatenate(as_source, axis=0)


def source_weights(pos, strength):
    weights = jnp.concatenate([strength, cross(pos, strength)], axis=0)
    high, low = cut(weights)
    rest = jnp.zeros((weight_rows - 12, pos.shape[1]), jnp.float32)
    return jnp.concatenate([high, low, rest], axis=0)


def kernel(
    n_tm,
    groups,
    table_q,
    small_ref,
    lists_ref,
    x_ref,
    a_ref,
    start_ref,
    live_ref,
    o_ref,
    own,
    stage,
    landed,
    table,
    targets,
    parts,
    totals,
    inc_out,
    inc_in,
    send_sem,
    recv_sem,
    inc_send_sem,
    inc_recv_sem,
):
    tm, me = lax.axis_index("tm"), lax.axis_index("space")
    columns = x_ref.shape[1]
    blocks = columns // block_size
    list_len = lists_ref.shape[0] // blocks
    n_chunks = blocks // chunk_blocks
    chunk = chunk_blocks * block_size

    barrier = pltpu.get_barrier_semaphore()
    for d in range(1, groups):
        peer = lax.rem(me + d, groups)
        pl.semaphore_signal(barrier, inc=1, device_id=(tm, peer), device_id_type=MESH)
    for d in range(1, n_tm):
        peer = lax.rem(tm + d, n_tm)
        pl.semaphore_signal(barrier, inc=1, device_id=(peer, me), device_id_type=MESH)

    def block_at(index):
        return pl.ds(pl.multiple_of(index * block_size, block_size), block_size)

    for block in range(blocks):
        lanes = slice(block * block_size, (block + 1) * block_size)
        own[block, 0:9] = x_ref[:, lanes]
        own[block, 9:12] = a_ref[:, lanes]
    for d in range(1, groups):
        peer = lax.rem(me + d, groups)
        for k in range(CAP):
            lanes = slice(k * block_size, (k + 1) * block_size)
            stage[d, :, lanes] = own[small_ref[k * groups + peer]]

    pl.semaphore_wait(barrier, groups - 1 + n_tm - 1)

    def sources_copy(d):
        return pltpu.make_async_remote_copy(
            src_ref=stage.at[d],
            dst_ref=landed.at[d],
            send_sem=send_sem.at[d],
            recv_sem=recv_sem.at[d],
            device_id=(tm, lax.rem(me + d, groups)),
            device_id_type=MESH,
        )

    for d in range(1, groups):
        sources_copy(d).start()

    centre = jnp.sum(x_ref[...], axis=1, keepdims=True) * (1.0 / columns)

    def enter(slot, count, pos, strength):
        here = [pos[3 * node : 3 * node + 3] for node in range(3)]
        pairs = [features(place) for place in here]
        weights = [source_weights(place, strength) for place in here]
        rows = [as_source for _, as_source in pairs] + weights
        rows = jnp.concatenate(rows, axis=0).astype(jnp.bfloat16)
        for k in range(count):
            table[slot + k] = rows[:, k * block_size : (k + 1) * block_size]
        return jnp.concatenate([as_target for as_target, _ in pairs], axis=0)

    own_step = 4

    def enter_own(step, carry):
        span = pl.ds(
            pl.multiple_of(step * own_step * block_size, block_size), own_step * block_size
        )
        pos = x_ref[:, span] - centre
        targets[:, span] = enter(step * own_step, own_step, pos, a_ref[:, span])
        return carry

    lax.fori_loop(0, blocks // own_step, enter_own, 0)

    for d in range(1, groups):
        sources_copy(d).wait()

    def enter_landed(step, carry):
        pos = landed[step, 0:9, :] - centre
        enter(blocks + (step - 1) * CAP, CAP, pos, landed[step, 9:12, :])
        return carry

    lax.fori_loop(1, groups, enter_landed, 0)

    def inc_copy(d, part):
        return pltpu.make_async_remote_copy(
            src_ref=inc_out.at[part],
            dst_ref=inc_in.at[d, part],
            send_sem=inc_send_sem.at[d, part],
            recv_sem=inc_recv_sem.at[d, part],
            device_id=(lax.rem(tm + d, n_tm), me),
            device_id_type=MESH,
        )

    def interact(block, buffer, beside):
        slots = [lists_ref[block * list_len + j] for j in range(list_len)]
        here = block_at(block)
        turned = targets[:, here].T
        node_of = lax.broadcasted_iota(jnp.int32, turned.shape, 1) // feature_rows
        lhs = [jnp.where(node_of == node, turned, 0.0) for node in range(3)]
        lhs = jnp.concatenate(lhs, axis=0).astype(jnp.bfloat16)
        for j in range(0, list_len, 2):
            pair = [table[slot, : 3 * feature_rows] for slot in slots[j : j + 2]]
            distance = jnp.dot(
                lhs, jnp.concatenate(pair, axis=1), preferred_element_type=jnp.float32
            )
            inverse = lax.rsqrt(distance)
            value = inverse * inverse * inverse
            high = value.astype(jnp.bfloat16)
            low = (value - high.astype(jnp.float32)).astype(jnp.bfloat16)
            lanes = slice(j * block_size, (j + 2) * block_size)
            parts[buffer, : 3 * block_size, lanes] = high
            parts[buffer, 3 * block_size :, lanes] = low
            beside(j // 2)

    def weigh(block, buffer):
        slots = [lists_ref[block * list_len + j] for j in range(list_len)]
        here = block_at(block)
        weights = [table[slot, 3 * feature_rows :] for slot in slots]
        weights = jnp.concatenate(weights, axis=1)
        node_of = lax.broadcasted_iota(jnp.int32, (block_size, 3 * weight_rows), 1) // weight_rows
        sums = []

        def part(index):
            if index >= 6:
                return
            rows = slice(index * block_size, (index + 1) * block_size)
            sums.append(
                lax.dot_general(
                    parts[buffer, rows],
                    weights,
                    (((1,), (1,)), ((), ())),
                    preferred_element_type=jnp.float32,
                )
            )
            if index == 5:
                kept = jnp.zeros((block_size, 3 * weight_rows), jnp.float32)
                for node in range(3):
                    kept = jnp.where(node_of == node, sums[node] + sums[node + 3], kept)
                totals[:, here] = kept.T

        return part

    def two_blocks(step, carry):
        interact(2 * step + 1, 1, weigh(2 * step, 0))
        interact(jnp.minimum(2 * step + 2, blocks - 1), 0, weigh(2 * step + 1, 1))
        return carry

    def one_chunk(part, carry):
        steps = chunk_blocks // 2
        lax.fori_loop(part * steps, (part + 1) * steps, two_blocks, 0)
        span = pl.ds(pl.multiple_of(part * chunk, block_size), chunk)
        scale = live_ref[:, span] * (-0.25 / math.pi)
        rates = []
        for node in range(3):
            rows = slice(3 * node, 3 * node + 3)
            pos = x_ref[rows, span] - centre[rows]
            sums = totals[weight_rows * node : weight_rows * (node + 1), span]
            spread = cross(pos, sums[0:3] + sums[6:9]) - (sums[3:6] + sums[9:12])
            rates.append(spread * scale)
        start = start_ref[:, span]
        for node in range(3):
            quadrature = step_size * (
                table_q[node][0] * rates[0]
                + table_q[node][1] * rates[1]
                + table_q[node][2] * rates[2]
            )
            o_ref[3 * node : 3 * node + 3, span] = start + quadrature
        inc_out[part] = quadrature
        for d in range(1, n_tm):

            @pl.when(tm + d < n_tm)
            def _():
                inc_copy(d, part).start()

        return carry

    interact(0, 0, lambda part: None)
    lax.fori_loop(0, n_chunks, one_chunk, 0)

    def finish(part, carry):
        span = pl.ds(pl.multiple_of(part * chunk, block_size), chunk)
        for d in range(1, n_tm):

            @pl.when(tm + d < n_tm)
            def _():
                inc_copy(d, part).wait_send()

            @pl.when(tm - d >= 0)
            def _():
                inc_copy(d, part).wait_recv()
                arrived = inc_in[d, part]
                for node in range(3):
                    rows = slice(3 * node, 3 * node + 3)
                    o_ref[rows, span] = o_ref[rows, span] + arrived

        return carry

    lax.fori_loop(0, n_chunks, finish, 0)


def shards(node_states, strengths, start_state, lists, counts):
    n_tm, groups = lax.axis_size("tm"), lax.axis_size("space")
    me = lax.axis_index("space")
    blocks = lists.shape[0] // groups
    columns = node_states.shape[2]
    n_chunks = blocks // chunk_blocks
    slots = blocks + (groups - 1) * CAP

    by_shard = lists.reshape(groups, -1)
    owner = by_shard // blocks
    local = by_shard - me * blocks
    asked = owner == me
    first = jnp.min(jnp.where(asked, local, blocks - 1), axis=1)
    last = jnp.max(jnp.where(asked, local, 0), axis=1)
    my_lists = lax.dynamic_index_in_dim(by_shard, me, 0, keepdims=False)
    shard_ids = jnp.arange(groups, dtype=jnp.int32)[:, None]
    lowest = jnp.min(
        jnp.where(my_lists[None] // blocks == shard_ids, my_lists[None], lists.shape[0]), axis=1
    )
    small = jnp.concatenate([first, last])
    shard = my_lists // blocks
    low = jnp.sum(jnp.where(shard[None] == shard_ids, lowest[:, None], 0), axis=0)
    away = (me - shard + groups) % groups
    my_slots = jnp.where(
        shard == me,
        my_lists - me * blocks,
        blocks + (away - 1) * CAP + (my_lists != low).astype(jnp.int32),
    )
    live_count = jnp.sum(jnp.where(jnp.arange(groups, dtype=jnp.int32) == me, counts, 0))
    live = jnp.arange(columns, dtype=jnp.int32)[None] < live_count * block_size

    chunk = chunk_blocks * block_size
    out = pl.pallas_call(
        functools.partial(kernel, n_tm, groups, radau_matrix().tolist()),
        out_shape=jax.ShapeDtypeStruct((9, columns), jnp.float32),
        in_specs=[pl.BlockSpec(memory_space=pltpu.SMEM)] * 2
        + [pl.BlockSpec(memory_space=pltpu.VMEM)] * 4,
        out_specs=pl.BlockSpec(memory_space=pltpu.VMEM),
        scratch_shapes=[
            pltpu.VMEM((blocks, 12, block_size), jnp.float32),
            pltpu.VMEM((groups, 12, CAP * block_size), jnp.float32),
            pltpu.VMEM((groups, 12, CAP * block_size), jnp.float32),
            pltpu.VMEM((slots, 3 * (feature_rows + weight_rows), block_size), jnp.bfloat16),
            pltpu.VMEM((3 * feature_rows, columns), jnp.float32),
            pltpu.VMEM((2, 6 * block_size, lists.shape[1] * block_size), jnp.bfloat16),
            pltpu.VMEM((3 * weight_rows, columns), jnp.float32),
            pltpu.VMEM((n_chunks, 3, chunk), jnp.float32),
            pltpu.VMEM((n_tm, n_chunks, 3, chunk), jnp.float32),
            pltpu.SemaphoreType.DMA((groups,)),
            pltpu.SemaphoreType.DMA((groups,)),
            pltpu.SemaphoreType.DMA((n_tm, n_chunks)),
            pltpu.SemaphoreType.DMA((n_tm, n_chunks)),
        ],
        compiler_params=pltpu.CompilerParams(
            collective_id=0, has_side_effects=True, vmem_limit_bytes=40 << 20
        ),
        name="vortex_window",
    )(small, my_slots, node_states[0], strengths, start_state, live.astype(jnp.float32))
    return out.reshape(1, 9, -1)


def solution(mesh):
    return jax.shard_map(
        shards,
        mesh=mesh,
        in_specs=(P("tm", None, "space"), P(None, "space"), P(None, "space"), P(), P()),
        out_specs=P("tm", None, "space"),
        check_vma=False,
    )
```

```python
import functools
import math

import jax
import jax.numpy as jnp
import numpy as np
from jax import lax
from jax.experimental import pallas as pl
from jax.experimental.pallas import tpu as pltpu
from jax.sharding import PartitionSpec as P

core_sq = 0.25
step_size = 1.0
block_size = 128
CAP = 2
feature_rows = 32
weight_rows = 16
chunk_blocks = 8
direct_pairs = (1, 3, 5)
MESH = pl.DeviceIdType.MESH


def radau_matrix():
    sqrt_six = math.sqrt(6.0)
    return np.array(
        [
            [
                (88.0 - 7.0 * sqrt_six) / 360.0,
                (296.0 - 169.0 * sqrt_six) / 1800.0,
                (-2.0 + 3.0 * sqrt_six) / 225.0,
            ],
            [
                (296.0 + 169.0 * sqrt_six) / 1800.0,
                (88.0 + 7.0 * sqrt_six) / 360.0,
                (-2.0 - 3.0 * sqrt_six) / 225.0,
            ],
            [(16.0 - sqrt_six) / 36.0, (16.0 + sqrt_six) / 36.0, 1.0 / 9.0],
        ]
    )


def cut(value):
    head = value.astype(jnp.bfloat16).astype(jnp.float32)
    return head, value - head


def cut_thrice(value):
    high, rest = cut(value)
    middle, low = cut(rest)
    return high, middle, low


def cross(former, latter):
    return jnp.concatenate(
        [
            former[1:2] * latter[2:3] - former[2:3] * latter[1:2],
            former[2:3] * latter[0:1] - former[0:1] * latter[2:3],
            former[0:1] * latter[1:2] - former[1:2] * latter[0:1],
        ],
        axis=0,
    )


def features(pos):
    high, middle, low = cut_thrice(pos)
    square = jnp.sum(pos * pos, axis=0, keepdims=True)
    ones = jnp.ones((3, pos.shape[1]), jnp.float32)
    rest = jnp.zeros((feature_rows - 24, pos.shape[1]), jnp.float32)
    as_target = [high, high, middle, middle, high, low, ones, *cut_thrice(square), rest]
    as_source = [
        high * -2.0,
        middle * -2.0,
        high * -2.0,
        middle * -2.0,
        low * -2.0,
        high * -2.0,
        *cut_thrice(square + core_sq),
        ones,
        rest,
    ]
    return jnp.concatenate(as_target, axis=0), jnp.concatenate(as_source, axis=0)


def source_weights(pos, strength):
    weights = jnp.concatenate([strength, cross(pos, strength)], axis=0)
    high, low = cut(weights)
    rest = jnp.zeros((weight_rows - 12, pos.shape[1]), jnp.float32)
    return jnp.concatenate([high, low, rest], axis=0)


def kernel(
    n_tm,
    groups,
    table_q,
    small_ref,
    lists_ref,
    x_ref,
    a_ref,
    start_ref,
    live_ref,
    o_ref,
    own,
    stage,
    landed,
    table,
    places,
    targets,
    parts,
    totals,
    inc_out,
    inc_in,
    send_sem,
    recv_sem,
    inc_send_sem,
    inc_recv_sem,
):
    tm, me = lax.axis_index("tm"), lax.axis_index("space")
    columns = x_ref.shape[1]
    blocks = columns // block_size
    list_len = lists_ref.shape[0] // blocks
    n_chunks = blocks // chunk_blocks
    chunk = chunk_blocks * block_size

    barrier = pltpu.get_barrier_semaphore()
    for d in range(1, groups):
        peer = lax.rem(me + d, groups)
        pl.semaphore_signal(barrier, inc=1, device_id=(tm, peer), device_id_type=MESH)
    for d in range(1, n_tm):
        peer = lax.rem(tm + d, n_tm)
        pl.semaphore_signal(barrier, inc=1, device_id=(peer, me), device_id_type=MESH)

    def block_at(index):
        return pl.ds(pl.multiple_of(index * block_size, block_size), block_size)

    for block in range(blocks):
        lanes = slice(block * block_size, (block + 1) * block_size)
        own[block, 0:9] = x_ref[:, lanes]
        own[block, 9:12] = a_ref[:, lanes]
    for d in range(1, groups):
        peer = lax.rem(me + d, groups)
        for k in range(CAP):
            lanes = slice(k * block_size, (k + 1) * block_size)
            stage[d, :, lanes] = own[small_ref[k * groups + peer]]

    pl.semaphore_wait(barrier, groups - 1 + n_tm - 1)

    def sources_copy(d):
        return pltpu.make_async_remote_copy(
            src_ref=stage.at[d],
            dst_ref=landed.at[d],
            send_sem=send_sem.at[d],
            recv_sem=recv_sem.at[d],
            device_id=(tm, lax.rem(me + d, groups)),
            device_id_type=MESH,
        )

    for d in range(1, groups):
        sources_copy(d).start()

    centre = jnp.sum(x_ref[...], axis=1, keepdims=True) * (1.0 / columns)

    def enter(slot, count, pos, strength):
        here = [pos[3 * node : 3 * node + 3] for node in range(3)]
        pairs = [features(place) for place in here]
        weights = [source_weights(place, strength) for place in here]
        rows = [as_source for _, as_source in pairs] + weights
        rows = jnp.concatenate(rows, axis=0).astype(jnp.bfloat16)
        for k in range(count):
            lanes = slice(k * block_size, (k + 1) * block_size)
            table[slot + k] = rows[:, lanes]
            places[slot + k] = pos[:, lanes]
        return jnp.concatenate([as_target for as_target, _ in pairs], axis=0)

    own_step = 4

    def enter_own(step, carry):
        span = pl.ds(
            pl.multiple_of(step * own_step * block_size, block_size), own_step * block_size
        )
        pos = x_ref[:, span] - centre
        targets[:, span] = enter(step * own_step, own_step, pos, a_ref[:, span])
        return carry

    lax.fori_loop(0, blocks // own_step, enter_own, 0)

    for d in range(1, groups):
        sources_copy(d).wait()

    def enter_landed(step, carry):
        pos = landed[step, 0:9, :] - centre
        enter(blocks + (step - 1) * CAP, CAP, pos, landed[step, 9:12, :])
        return carry

    lax.fori_loop(1, groups, enter_landed, 0)

    def inc_copy(d, part):
        return pltpu.make_async_remote_copy(
            src_ref=inc_out.at[part],
            dst_ref=inc_in.at[d, part],
            send_sem=inc_send_sem.at[d, part],
            recv_sem=inc_recv_sem.at[d, part],
            device_id=(lax.rem(tm + d, n_tm), me),
            device_id_type=MESH,
        )

    def direct(spots, sources):
        rows = []
        for node in range(3):
            distance = core_sq
            for c in range(3 * node, 3 * node + 3):
                offset = spots[c] - sources[c : c + 1]
                distance = offset * offset + distance
            rows.append(distance)
        return jnp.concatenate(rows, axis=0)

    def interact(block, buffer, beside):
        slots = [lists_ref[block * list_len + j] for j in range(list_len)]
        here = block_at(block)
        turned = targets[:, here].T
        node_of = lax.broadcasted_iota(jnp.int32, turned.shape, 1) // feature_rows
        lhs = [jnp.where(node_of == node, turned, 0.0) for node in range(3)]
        lhs = jnp.concatenate(lhs, axis=0).astype(jnp.bfloat16)
        own_places = places[block].T
        spots = [
            jnp.broadcast_to(own_places[:, row : row + 1], (block_size, block_size))
            for row in range(9)
        ]
        for j in range(0, list_len, 2):
            if j // 2 in direct_pairs:
                distance = [direct(spots, places[slot]) for slot in slots[j : j + 2]]
                distance = jnp.concatenate(distance, axis=1)
            else:
                pair = [table[slot, : 3 * feature_rows] for slot in slots[j : j + 2]]
                distance = jnp.dot(
                    lhs, jnp.concatenate(pair, axis=1), preferred_element_type=jnp.float32
                )
            inverse = lax.rsqrt(distance)
            value = inverse * inverse * inverse
            high = value.astype(jnp.bfloat16)
            low = (value - high.astype(jnp.float32)).astype(jnp.bfloat16)
            lanes = slice(j * block_size, (j + 2) * block_size)
            parts[buffer, : 3 * block_size, lanes] = high
            parts[buffer, 3 * block_size :, lanes] = low
            beside(j // 2)

    def weigh(block, buffer):
        slots = [lists_ref[block * list_len + j] for j in range(list_len)]
        here = block_at(block)
        weights = [table[slot, 3 * feature_rows :] for slot in slots]
        weights = jnp.concatenate(weights, axis=1)
        node_of = lax.broadcasted_iota(jnp.int32, (block_size, 3 * weight_rows), 1) // weight_rows
        sums = []

        def part(index):
            if index >= 6:
                return
            rows = slice(index * block_size, (index + 1) * block_size)
            sums.append(
                lax.dot_general(
                    parts[buffer, rows],
                    weights,
                    (((1,), (1,)), ((), ())),
                    preferred_element_type=jnp.float32,
                )
            )
            if index == 5:
                kept = jnp.zeros((block_size, 3 * weight_rows), jnp.float32)
                for node in range(3):
                    kept = jnp.where(node_of == node, sums[node] + sums[node + 3], kept)
                totals[:, here] = kept.T

        return part

    def two_blocks(step, carry):
        interact(2 * step + 1, 1, weigh(2 * step, 0))
        interact(jnp.minimum(2 * step + 2, blocks - 1), 0, weigh(2 * step + 1, 1))
        return carry

    def one_chunk(part, carry):
        steps = chunk_blocks // 2
        lax.fori_loop(part * steps, (part + 1) * steps, two_blocks, 0)
        span = pl.ds(pl.multiple_of(part * chunk, block_size), chunk)
        scale = live_ref[:, span] * (-0.25 / math.pi)
        rates = []
        for node in range(3):
            rows = slice(3 * node, 3 * node + 3)
            pos = x_ref[rows, span] - centre[rows]
            sums = totals[weight_rows * node : weight_rows * (node + 1), span]
            spread = cross(pos, sums[0:3] + sums[6:9]) - (sums[3:6] + sums[9:12])
            rates.append(spread * scale)
        start = start_ref[:, span]
        for node in range(3):
            quadrature = step_size * (
                table_q[node][0] * rates[0]
                + table_q[node][1] * rates[1]
                + table_q[node][2] * rates[2]
            )
            o_ref[3 * node : 3 * node + 3, span] = start + quadrature
        inc_out[part] = quadrature
        for d in range(1, n_tm):

            @pl.when(tm + d < n_tm)
            def _():
                inc_copy(d, part).start()

        return carry

    interact(0, 0, lambda part: None)
    lax.fori_loop(0, n_chunks, one_chunk, 0)

    def finish(part, carry):
        span = pl.ds(pl.multiple_of(part * chunk, block_size), chunk)
        for d in range(1, n_tm):

            @pl.when(tm + d < n_tm)
            def _():
                inc_copy(d, part).wait_send()

            @pl.when(tm - d >= 0)
            def _():
                inc_copy(d, part).wait_recv()
                arrived = inc_in[d, part]
                for node in range(3):
                    rows = slice(3 * node, 3 * node + 3)
                    o_ref[rows, span] = o_ref[rows, span] + arrived

        return carry

    lax.fori_loop(0, n_chunks, finish, 0)


def shards(node_states, strengths, start_state, lists, counts):
    n_tm, groups = lax.axis_size("tm"), lax.axis_size("space")
    me = lax.axis_index("space")
    blocks = lists.shape[0] // groups
    columns = node_states.shape[2]
    n_chunks = blocks // chunk_blocks
    slots = blocks + (groups - 1) * CAP

    by_shard = lists.reshape(groups, -1)
    owner = by_shard // blocks
    local = by_shard - me * blocks
    asked = owner == me
    first = jnp.min(jnp.where(asked, local, blocks - 1), axis=1)
    last = jnp.max(jnp.where(asked, local, 0), axis=1)
    my_lists = lax.dynamic_index_in_dim(by_shard, me, 0, keepdims=False)
    shard_ids = jnp.arange(groups, dtype=jnp.int32)[:, None]
    lowest = jnp.min(
        jnp.where(my_lists[None] // blocks == shard_ids, my_lists[None], lists.shape[0]), axis=1
    )
    small = jnp.concatenate([first, last])
    shard = my_lists // blocks
    low = jnp.sum(jnp.where(shard[None] == shard_ids, lowest[:, None], 0), axis=0)
    away = (me - shard + groups) % groups
    my_slots = jnp.where(
        shard == me,
        my_lists - me * blocks,
        blocks + (away - 1) * CAP + (my_lists != low).astype(jnp.int32),
    )
    live_count = jnp.sum(jnp.where(jnp.arange(groups, dtype=jnp.int32) == me, counts, 0))
    live = jnp.arange(columns, dtype=jnp.int32)[None] < live_count * block_size

    chunk = chunk_blocks * block_size
    out = pl.pallas_call(
        functools.partial(kernel, n_tm, groups, radau_matrix().tolist()),
        out_shape=jax.ShapeDtypeStruct((9, columns), jnp.float32),
        in_specs=[pl.BlockSpec(memory_space=pltpu.SMEM)] * 2
        + [pl.BlockSpec(memory_space=pltpu.VMEM)] * 4,
        out_specs=pl.BlockSpec(memory_space=pltpu.VMEM),
        scratch_shapes=[
            pltpu.VMEM((blocks, 12, block_size), jnp.float32),
            pltpu.VMEM((groups, 12, CAP * block_size), jnp.float32),
            pltpu.VMEM((groups, 12, CAP * block_size), jnp.float32),
            pltpu.VMEM((slots, 3 * (feature_rows + weight_rows), block_size), jnp.bfloat16),
            pltpu.VMEM((slots, 9, block_size), jnp.float32),
            pltpu.VMEM((3 * feature_rows, columns), jnp.float32),
            pltpu.VMEM((2, 6 * block_size, lists.shape[1] * block_size), jnp.bfloat16),
            pltpu.VMEM((3 * weight_rows, columns), jnp.float32),
            pltpu.VMEM((n_chunks, 3, chunk), jnp.float32),
            pltpu.VMEM((n_tm, n_chunks, 3, chunk), jnp.float32),
            pltpu.SemaphoreType.DMA((groups,)),
            pltpu.SemaphoreType.DMA((groups,)),
            pltpu.SemaphoreType.DMA((n_tm, n_chunks)),
            pltpu.SemaphoreType.DMA((n_tm, n_chunks)),
        ],
        compiler_params=pltpu.CompilerParams(
            collective_id=0, has_side_effects=True, vmem_limit_bytes=40 << 20
        ),
        name="vortex_window",
    )(small, my_slots, node_states[0], strengths, start_state, live.astype(jnp.float32))
    return out.reshape(1, 9, -1)


def solution(mesh):
    return jax.shard_map(
        shards,
        mesh=mesh,
        in_specs=(P("tm", None, "space"), P(None, "space"), P(None, "space"), P(), P()),
        out_specs=P("tm", None, "space"),
        check_vma=False,
    )
```
